32 devices in a mesh: seq: 8 (over z, x), head: 4 (over y, core).
Axes of the slice: x: 2, y: 2, z: 4, core: 2. Of those that a mesh axis runs over, the one named last changes fastest.
Arguments:
- tokens: bfloat16 [4096, 4096], P(('seq', 'head')), may hold values from -6 to 6
- in_weight: bfloat16 [4096, 8192], P('seq', 'head'), may hold values from -0.09375 to 0.09375
- write_proj: bfloat16 [4096, 128], P(('seq', 'head')), may hold values from -6 to 6
- read_proj: bfloat16 [4096, 128], P(('seq', 'head')), may hold values from -0.5 to 0.5
- log_decay: float32 [128, 4096], P('head', 'seq'), may hold values from -1.1 to 0, as said below
- level_gain: float32 [7, 128, 4096], P(None, 'head', 'seq'), may hold values from 0 to 1, as said below
- out_grad: bfloat16 [4096, 8192], P('seq', 'head'), may hold values from -6 to 6
Outputs:
- layer_out: bfloat16 [4096, 8192], P('seq', 'head')
- weight_grad: bfloat16 [4096, 8192], P('seq', 'head')
The draws below stay inside these ranges and needn't reach their ends.
Inputs may be any that keep to these rules, and one draw needn't show every extreme that they name: `log_decay`: Log-decays are non-positive. `level_gain`: level weights are positive.
All inputs are finite; a program needn't handle non-finite values.
Results may differ from the reference program's by a relative error of at most 0.02.
Values may be sent and summed in bfloat16 or wider, within the bound.
A program may use at most 128 MiB of HBM per device.

```python
import math
import jax
import jax.numpy as jnp
from jax import lax

D = 4096
HEAD_COUNT = 128
HEAD_DIM = 64
STATE = 128
CH = 64
TOK_DEV = 512
TOKEN_COUNT = 4096
LOCAL_LEVELS = 4
SEQ_LEVELS = 3
LEVELS = 7
N_SEQ = 8


def draw_log_decay(key, part):
    random_keys = jax.random.split(key, 7)
    fast_share = 0.5
    rough_low = 0.5
    rough_high = 1.5
    is_fast = jax.random.uniform(random_keys[0], (HEAD_COUNT,)) < fast_share
    fast_rate = jax.random.uniform(random_keys[1], (HEAD_COUNT,), minval=1.0 / 50.0, maxval=1.0 / 30.0)
    slow_rate = jnp.exp(jax.random.uniform(random_keys[2], (HEAD_COUNT,), minval=math.log(0.03), maxval=math.log(0.4))) / TOKEN_COUNT
    decay_speed = jnp.where(is_fast, fast_rate, slow_rate)
    segment_count = TOKEN_COUNT // TOK_DEV
    multiplier = jax.random.uniform(random_keys[3], (HEAD_COUNT, segment_count), minval=0.5, maxval=1.5)
    multiplier = jnp.repeat(multiplier, TOK_DEV, axis=1)
    jaggedness = jax.random.uniform(random_keys[4], (HEAD_COUNT, TOKEN_COUNT), minval=rough_low, maxval=rough_high)
    spike_position = jax.random.randint(random_keys[5], (HEAD_COUNT, 2, 1), 0, TOKEN_COUNT)
    spike_loss = jnp.log(jax.random.uniform(random_keys[6], (HEAD_COUNT, 2, 1), minval=0.6, maxval=0.8))
    token_position = jnp.arange(TOKEN_COUNT, dtype=jnp.int32)[None, None, :]
    spike_events = jnp.sum(jnp.where(token_position == spike_position, spike_loss, 0.0), axis=1)
    return (-decay_speed[:, None] * multiplier * jaggedness + spike_events).astype(jnp.float32)


def draw_level_gain(key, part):
    number = jnp.arange(LEVELS)
    level_span = CH * jnp.exp2(jnp.maximum(number - 1, 0).astype(jnp.float32))
    jaggedness = jax.random.uniform(key, (LEVELS, HEAD_COUNT, TOKEN_COUNT), minval=0.3, maxval=1.2)
    return (jaggedness / jnp.sqrt(level_span)[:, None, None]).astype(jnp.float32)


def raised(values, own_key, source, target, shards_of, factor):
    def block_of(axis_at):
        return (jnp.arange(values.shape[axis_at]) // (values.shape[axis_at] // shards_of)).reshape((-1,) + (1,) * (values.ndim - 1 - axis_at))

    one_side = jax.random.permutation(own_key, shards_of)[block_of(target)]
    other_side = (block_of(target) + shards_of // 2) % shards_of
    return jnp.where((block_of(source) == one_side) | (block_of(source) == other_side), factor * values, values)


def block_levels(rng, dims, cuts, least, top_value):
    level, own = 1.0, jax.random.fold_in(rng, 6)
    for axis_at, parts in cuts:
        draws = jnp.exp(jax.random.uniform(jax.random.fold_in(own, axis_at), (parts,), jnp.float32, least / len(cuts), top_value / len(cuts)))
        level = level * jnp.repeat(draws, dims[axis_at] // parts).reshape([-1 if axis == axis_at else 1 for axis in range(len(dims))])
    return level


def noise(rng, dims, spread, limit, cuts=(), kind=jnp.bfloat16):
    level = block_levels(rng, dims, cuts, -0.22, 0.18) if cuts else 1.0
    entries = jax.random.normal(rng, dims, jnp.float32) * spread * level
    return jnp.minimum(jnp.maximum(entries, -limit), limit).astype(kind)


def heavy_noise(key, shape, width, bound, cuts, heavy, kind=jnp.bfloat16):
    drawn = width * jax.random.normal(key, shape, jnp.float32)
    if cuts:
        drawn = drawn * block_levels(key, shape, cuts, -0.22, 0.18)
    return jnp.clip(raised(drawn, jax.random.fold_in(key, 3), *heavy), -bound, bound).astype(kind)


def setup_inputs(seed: int = 0) -> dict:
    keys = jax.random.split(jax.random.key(seed), 8)
    tokens = heavy_noise(keys[0], (TOKEN_COUNT, D), 1.0, 6.0, ((0, 32),), (0, 1, 32, 2.75))
    in_weight = noise(keys[1], (D, HEAD_COUNT * HEAD_DIM), D ** -0.5, 0.09375, ((0, 8), (1, 4)))
    write_proj = noise(keys[2], (TOKEN_COUNT, STATE), 1.0, 6.0, ((0, 32),))
    read_proj = noise(keys[3], (TOKEN_COUNT, STATE), STATE ** -0.5, 0.5, ((0, 32),))
    log_decay = draw_log_decay(jax.random.fold_in(keys[7], 71), 0)
    level_gain = draw_level_gain(jax.random.fold_in(keys[7], 71), 0)
    out_grad = noise(keys[6], (TOKEN_COUNT, HEAD_COUNT * HEAD_DIM), 1.0, 6.0, ((0, 8), (1, 4)))
    return dict(tokens=tokens, in_weight=in_weight, write_proj=write_proj, read_proj=read_proj, log_decay=log_decay, level_gain=level_gain, out_grad=out_grad)


def stretch_levels(length, level_count):
    stretches = jnp.arange(length, dtype=jnp.int32) // CH
    level_table = jnp.zeros((length, length), jnp.int32)
    for offset in range(level_count - 1):
        level_table = level_table + ((stretches[:, None] >> offset) != (stretches[None, :] >> offset)).astype(jnp.int32)
    return level_table


def head_terms(scores, level_table, causal, cumulative, gain_rows, values, grad_rows):
    gain_table = jnp.zeros(scores.shape, jnp.float32)
    for number in range(gain_rows.shape[0]):
        gain_table = gain_table + jnp.where(level_table == number, gain_rows[number][:, None], 0.0)
    differ = cumulative[:, None] - cumulative[None, :]
    decays = jnp.where(causal, jnp.exp(jnp.where(causal, differ, 0.0)), 0.0)
    weights = (gain_table * decays * scores).astype(jnp.bfloat16)
    forward = jnp.dot(weights, values, preferred_element_type=jnp.float32)
    backward = lax.dot_general(weights, grad_rows, (((0,), (0,)), ((), ())), preferred_element_type=jnp.float32)
    return forward, backward


def level_of(seg_index, order):
    differing = jnp.zeros(order.shape, jnp.int32)
    for offset in range(SEQ_LEVELS):
        differing = differing + ((seg_index >> offset) != (order >> offset)).astype(jnp.int32)
    return differing - 1


def make_keys(cumulative, totals, write_rows):
    scale_rows = jnp.exp(totals[:, None] - cumulative)
    return (scale_rows[:, :, None] * write_rows.astype(jnp.float32)[None]).astype(jnp.bfloat16)


def make_queries(cumulative, gain_rows, read_rows):
    scale_rows = gain_rows[LOCAL_LEVELS:] * jnp.exp(cumulative)[None]
    return (scale_rows[..., None] * read_rows.astype(jnp.float32)[None, None]).astype(jnp.bfloat16)


def to_half(array):
    return lax.optimization_barrier(array.astype(jnp.bfloat16)).astype(jnp.float32)


def reference(tokens, in_weight, write_proj, read_proj, log_decay, level_gain, out_grad):
    segments = N_SEQ
    inner_width = HEAD_COUNT * HEAD_DIM
    highest = lax.Precision.HIGHEST
    values = jnp.dot(tokens, in_weight, preferred_element_type=jnp.float32).astype(jnp.bfloat16)
    values_seg = values.reshape(segments, TOK_DEV, HEAD_COUNT, HEAD_DIM)
    tokens_seg = tokens.reshape(segments, TOK_DEV, D)
    write_seg = write_proj.reshape(segments, TOK_DEV, STATE)
    read_seg = read_proj.reshape(segments, TOK_DEV, STATE)
    cumulative = jnp.cumsum(log_decay.reshape(HEAD_COUNT, segments, TOK_DEV), axis=2).transpose(1, 0, 2)
    totals = cumulative[:, :, -1]
    gains_seg = level_gain.reshape(LEVELS, HEAD_COUNT, segments, TOK_DEV).transpose(2, 0, 1, 3)
    grads_seg = out_grad.reshape(segments, TOK_DEV, HEAD_COUNT, HEAD_DIM)

    def summarize(inputs):
        cum_rows, total_rows, write_rows, read_rows, value_rows, gain_rows, grad_rows = inputs
        key_rows = make_keys(cum_rows, total_rows, write_rows)
        seg_state = jnp.einsum('htn,thp->hnp', key_rows.astype(jnp.float32), value_rows.astype(jnp.float32), precision=highest)
        queries = make_queries(cum_rows, gain_rows, read_rows)
        level_grad = jnp.einsum('bhtn,thp->bhnp', queries.astype(jnp.float32), grad_rows.astype(jnp.float32), precision=highest)
        return seg_state, level_grad

    states, level_grads = lax.map(summarize, (cumulative, totals, write_seg, read_seg, values_seg, gains_seg, grads_seg))
    running = jnp.cumsum(totals, axis=0)
    before = running - totals
    order = jnp.arange(segments, dtype=jnp.int32)
    level_table = stretch_levels(TOK_DEV, LOCAL_LEVELS)
    steps_idx = jnp.arange(TOK_DEV, dtype=jnp.int32)
    causal = steps_idx[:, None] >= steps_idx[None, :]

    def segment_step(accumulated, inputs):
        seg_index, cum_rows, total_rows, write_rows, read_rows, value_rows, gain_rows, grad_rows, token_rows = inputs
        levels_seg = level_of(seg_index, order)
        is_earlier = (order < seg_index)[:, None]
        is_later = (order > seg_index)[:, None]
        to_here = jnp.where(is_earlier, jnp.exp(jnp.where(is_earlier, before[seg_index][None, :] - running, 0.0)), 0.0)
        from_here = jnp.where(is_later, jnp.exp(jnp.where(is_later, before - running[seg_index][None, :], 0.0)), 0.0)
        onehot = (levels_seg[None, :] == jnp.arange(SEQ_LEVELS, dtype=jnp.int32)[:, None]).astype(jnp.float32)
        buckets = jnp.einsum('bj,jh,jhnp->bhnp', onehot, to_here, states, precision=highest)
        state_grad = jnp.einsum('bk,kh,kbhnp->hnp', onehot, from_here, level_grads, precision=highest)
        bucket_half = to_half(buckets)
        state_half = to_half(state_grad)
        queries = make_queries(cum_rows, gain_rows, read_rows)
        cross_term = jnp.einsum('bhtn,bhnp->thp', queries.astype(jnp.float32), bucket_half, precision=highest)
        key_rows = make_keys(cum_rows, total_rows, write_rows)
        cross_grad = jnp.einsum('htn,hnp->thp', key_rows.astype(jnp.float32), state_half, precision=highest)
        scores = lax.dot_general(read_rows, write_rows, (((1,), (1,)), ((), ())), preferred_element_type=jnp.float32)

        def one_head(packed):
            cum_head, gain_head, value_head, grad_head = packed
            return head_terms(scores, level_table, causal, cum_head, gain_head, value_head, grad_head)

        local_out, local_grad = lax.map(one_head, (cum_rows, gain_rows[:LOCAL_LEVELS].transpose(1, 0, 2), value_rows.transpose(1, 0, 2), grad_rows.transpose(1, 0, 2)))
        layer_seg = (cross_term + local_out.transpose(1, 0, 2)).astype(jnp.bfloat16).reshape(TOK_DEV, inner_width)
        values_grad = (cross_grad + local_grad.transpose(1, 0, 2)).astype(jnp.bfloat16).reshape(TOK_DEV, inner_width)
        partial_grad = lax.dot_general(token_rows, values_grad, (((0,), (0,)), ((), ())), preferred_element_type=jnp.float32).astype(jnp.bfloat16)
        return accumulated + partial_grad.astype(jnp.float32), layer_seg

    start_sum = jnp.zeros((D, inner_width), jnp.float32)
    accumulated, layers = lax.scan(segment_step, start_sum, (order, cumulative, totals, write_seg, read_seg, values_seg, gains_seg, grads_seg, tokens_seg))
    return layers.reshape(TOKEN_COUNT, inner_width), accumulated.astype(jnp.bfloat16)
```

```python
import functools

import jax
import jax.numpy as jnp
from jax import lax
from jax.experimental import pallas as pl
from jax.experimental.pallas import tpu as pltpu
from jax.sharding import PartitionSpec as P

HEAD_DIM = 64
STATE = 128
CH = 64
TILE = 2 * CH
GROUP = 4


def swapped(value, axis, apart):
    mask = 2**apart
    pairs = [(source, source ^ mask) for source in range(lax.axis_size(axis))]
    return lax.ppermute(value, axis, pairs)


def dot32(left, right):
    return jnp.dot(left, right, preferred_element_type=jnp.float32)


def spread(cols, quantity, quantities, group, rows=slice(None)):
    parts = []
    count = rows.stop - rows.start if rows.start is not None else cols.shape[1]
    low = lax.broadcasted_iota(jnp.int32, (count, 2 * HEAD_DIM), 1) < HEAD_DIM
    for pair in range(group // 2):
        first, second = (2 * pair) * quantities + quantity, (2 * pair + 1) * quantities + quantity
        parts.append(
            jnp.where(low, cols[0, rows, first : first + 1], cols[0, rows, second : second + 1])
        )
    return jnp.concatenate(parts, axis=1)


def level_grad_kernel(names, group, read_t, grads, cols, out):
    count = len(names)
    for b in range(out.shape[0]):
        scaled = (spread(cols, names.index(("q", b)), count, group) * grads[...]).astype(jnp.bfloat16)
        out[b] = dot32(read_t[...], scaled)


def seg_state_kernel(names, group, write_t, values, cols, out):
    scaled = (spread(cols, names.index("key"), len(names), group) * values[...]).astype(jnp.bfloat16)
    out[...] = dot32(write_t[...], scaled)


def diagonal_terms(names, group, table, cols, rows, operand, rows_of, backward):
    count = len(names)
    position = slice(rows_of, rows_of + TILE)
    own = table[position, position].astype(jnp.float32)
    shape = (TILE, TILE)
    same = (lax.broadcasted_iota(jnp.int32, shape, 0) < CH) == (
        lax.broadcasted_iota(jnp.int32, shape, 1) < CH
    )
    parts = []
    for head in range(group):
        cum_col = cols[0, position, head * count : head * count + 1]
        cum_row = rows[0, 3 * head : 3 * head + 1, position]
        if backward:
            gain = jnp.where(
                same, rows[0, 3 * head + 1 : 3 * head + 2, position], rows[0, 3 * head + 2 : 3 * head + 3, position]
            )
            differ = cum_row - cum_col
        else:
            gain = jnp.where(
                same,
                cols[0, position, head * count + 1 : head * count + 2],
                cols[0, position, head * count + 2 : head * count + 3],
            )
            differ = cum_col - cum_row
        weights = (gain * jnp.exp(jnp.minimum(differ, 0.0)) * own).astype(jnp.bfloat16)
        parts.append(dot32(weights, operand[position, head * HEAD_DIM : (head + 1) * HEAD_DIM]))
    return jnp.concatenate(parts, axis=1)


def local_kernel(names, group, levels, backward, table, proj, operand, states, cols, rows, out):
    count = len(names)
    length = out.shape[0]
    tiles = length // TILE
    sums = []
    for tile in range(tiles):
        position = slice(tile * TILE, (tile + 1) * TILE)
        total = diagonal_terms(names, group, table, cols, rows, operand, tile * TILE, backward)
        if backward:
            total = total + spread(cols, names.index("key"), count, group, position) * dot32(
                proj[position, :], states[...]
            )
        else:
            for b in range(states.shape[0]):
                total = total + spread(cols, names.index(("q", b)), count, group, position) * dot32(
                    proj[position, :], states[b]
                )
        sums.append(total)
    for level in range(2, levels):
        half = CH << (level - 1)
        for start in range(0, length, 2 * half):
            lower, upper = slice(start, start + half), slice(start + half, start + 2 * half)
            source, target = (upper, lower) if backward else (lower, upper)
            inner, outer = ("r", "c") if backward else ("c", "r")
            scaled = (
                spread(cols, names.index((inner, level)), count, group, source) * operand[source, :]
            ).astype(jnp.bfloat16)
            term = spread(cols, names.index((outer, level)), count, group, target) * dot32(
                table[target, source], scaled
            )
            for step in range(half // TILE):
                at = target.start // TILE + step
                sums[at] = sums[at] + term[step * TILE : (step + 1) * TILE]
    for tile in range(tiles):
        out[tile * TILE : (tile + 1) * TILE, :] = sums[tile].astype(out.dtype)


def whole_spec(array):
    return pl.BlockSpec(array.shape, lambda i: (0,) * array.ndim)


def column_spec(array, width):
    lead = array.shape[:-1]
    return pl.BlockSpec(lead + (width,), lambda i: (0,) * len(lead) + (i,))


def group_spec(array):
    return pl.BlockSpec((1,) + array.shape[1:], lambda i: (i, 0, 0))


def call(kernel, groups, width, fixed, wide, grouped, out_shape, flops, name):
    out_lead = out_shape.shape[:-1]
    moved = sum(a.size * a.dtype.itemsize for a in (*fixed, *wide, *grouped))
    return pl.pallas_call(
        kernel,
        grid=(groups,),
        in_specs=[whole_spec(a) for a in fixed]
        + [column_spec(a, width) for a in wide]
        + [group_spec(a) for a in grouped],
        out_specs=pl.BlockSpec(out_lead + (width,), lambda i: (0,) * len(out_lead) + (i,)),
        out_shape=out_shape,
        compiler_params=pltpu.CompilerParams(vmem_limit_bytes=40 * 2**20),
        cost_estimate=pl.CostEstimate(flops=flops, bytes_accessed=moved, transcendentals=0),
        name=name,
    )(*fixed, *wide, *grouped)


def per_device(tokens, in_weight, write_proj, read_proj, log_decay, level_gain, out_grad):
    full_weight = lax.all_gather(in_weight, "seq", axis=0, tiled=True)
    both = lax.all_gather(jnp.concatenate([write_proj, read_proj], axis=1), "head", axis=0, tiled=True)
    write_rows, read_rows = both[:, :STATE], both[:, STATE:]
    full_tokens = lax.all_gather(tokens, "head", axis=0, tiled=True)
    tok_len = full_tokens.shape[0]
    head_count = log_decay.shape[0]
    columns = in_weight.shape[1]
    levels = (tok_len // CH).bit_length()
    seq_count = lax.axis_size("seq").bit_length() - 1
    me = lax.axis_index("seq")
    group = GROUP
    groups = head_count // group
    width = group * HEAD_DIM

    upper_ones = (jnp.arange(tok_len)[:, None] <= jnp.arange(tok_len)[None, :]).astype(jnp.float32)
    cumulative = jnp.dot(log_decay, upper_ones, precision=lax.Precision.HIGHEST)
    totals = cumulative[:, -1]
    all_totals = lax.all_gather(totals, "seq", axis=0, tiled=False)

    names = ["cum", "g0", "g1"]
    vectors = [cumulative, level_gain[0], level_gain[1]]
    for level in range(2, levels):
        half = CH << (level - 1)
        blocks = cumulative.reshape(head_count, tok_len // (2 * half), 2 * half)
        middle = blocks[:, :, half - 1 : half]
        after = jnp.exp(jnp.minimum(blocks - middle, 0.0)).reshape(head_count, tok_len)
        before = jnp.exp(jnp.minimum(middle - blocks, 0.0)).reshape(head_count, tok_len)
        names += [("r", level), ("c", level)]
        vectors += [level_gain[level] * after, before]
    names.append("key")
    vectors.append(jnp.exp(totals[:, None] - cumulative))
    grown = jnp.exp(cumulative)
    for b in range(seq_count):
        names.append(("q", b))
        vectors.append(level_gain[levels + b] * grown)
    names = tuple(names)
    count = len(names)
    cols = jnp.stack(vectors, axis=1).reshape(groups, group * count, tok_len).swapaxes(1, 2)
    rows = jnp.stack(vectors[:3], axis=1).reshape(groups, group * 3, tok_len)

    causal = jnp.arange(tok_len)[:, None] >= jnp.arange(tok_len)[None, :]
    scores = jnp.where(causal, dot32(read_rows, write_rows.T), 0.0).astype(jnp.bfloat16)
    scores_t = jnp.where(causal.T, dot32(write_rows, read_rows.T), 0.0).astype(jnp.bfloat16)

    work = 2 * tok_len * STATE * columns
    level_grads = call(
        functools.partial(level_grad_kernel, names, group),
        groups, width, [read_rows.T], [out_grad], [cols],
        jax.ShapeDtypeStruct((seq_count, STATE, columns), jnp.float32), seq_count * work, "level_grads",
    )

    index = jnp.arange(all_totals.shape[0])
    bit_flags = [me >> bit & 1 == 1 for bit in range(seq_count)]

    def per_column(vector):
        return jnp.repeat(vector, HEAD_DIM)[None, :]

    own_decays, partner_decays = [], []
    for bit in range(seq_count):
        for found, block in ((own_decays, me >> bit), (partner_decays, (me >> bit) ^ 1)):
            inside = (index >> bit == block)[:, None]
            found.append(per_column(jnp.exp(jnp.sum(jnp.where(inside, all_totals, 0.0), axis=0))))

    pending = [jnp.where(bit_flags[bit], level_grads[bit], 0.0) for bit in range(seq_count)]
    suffix = jnp.ones((1, columns), jnp.float32)
    state_grad = jnp.zeros((STATE, columns), jnp.float32)
    for bit in range(seq_count):
        partner = swapped(jnp.stack(pending[bit:]).astype(jnp.bfloat16), "seq", bit).astype(jnp.float32)
        is_upper = bit_flags[bit]
        state_grad = state_grad + jnp.where(is_upper, 0.0, suffix * partner[0])
        for later in range(bit + 1, seq_count):
            rest, other = pending[later], partner[later - bit]
            pending[later] = jnp.where(
                is_upper, other + partner_decays[bit] * rest, rest + own_decays[bit] * other
            )
        suffix = jnp.where(is_upper, suffix, suffix * partner_decays[bit])

    local_work = work + 2 * tok_len * tok_len * columns
    values_grad = call(
        functools.partial(local_kernel, names, group, levels, True),
        groups, width, [scores_t, write_rows], [out_grad, state_grad.astype(jnp.bfloat16)], [cols, rows],
        jax.ShapeDtypeStruct((tok_len, columns), jnp.bfloat16), local_work, "backward",
    )
    weight_grad = lax.psum_scatter(
        lax.dot_general(
            full_tokens, values_grad, (((0,), (0,)), ((), ())), preferred_element_type=jnp.float32
        ).astype(jnp.bfloat16),
        "seq", scatter_dimension=0, tiled=True,
    )

    values = dot32(full_tokens, full_weight).astype(jnp.bfloat16)
    block_state = call(
        functools.partial(seg_state_kernel, names, group),
        groups, width, [write_rows.T], [values], [cols],
        jax.ShapeDtypeStruct((STATE, columns), jnp.float32), work, "seg_state",
    )
    prefix = jnp.ones((1, columns), jnp.float32)
    buckets = []
    for bit in range(seq_count):
        partner = swapped(block_state.astype(jnp.bfloat16), "seq", bit).astype(jnp.float32)
        is_upper = bit_flags[bit]
        buckets.append(jnp.where(is_upper, prefix * partner, 0.0).astype(jnp.bfloat16))
        block_state = jnp.where(
            is_upper,
            own_decays[bit] * partner + block_state,
            partner_decays[bit] * block_state + partner,
        )
        prefix = jnp.where(is_upper, partner_decays[bit] * prefix, prefix)
    layer_out = call(
        functools.partial(local_kernel, names, group, levels, False),
        groups, width, [scores, read_rows], [values, jnp.stack(buckets)], [cols, rows],
        jax.ShapeDtypeStruct((tok_len, columns), jnp.bfloat16), local_work, "forward",
    )
    return (layer_out, weight_grad)


def solution(mesh):
    in_specs = (
        P(("seq", "head"), None),
        P("seq", "head"),
        P(("seq", "head"), None),
        P(("seq", "head"), None),
        P("head", "seq"),
        P(None, "head", "seq"),
        P("seq", "head"),
    )
    out_specs = (P("seq", "head"), P("seq", "head"))
    return jax.shard_map(
        per_device, mesh=mesh, in_specs=in_specs, out_specs=out_specs, check_vma=False
    )
```

```python
import functools

import jax
import jax.numpy as jnp
from jax import lax
from jax.experimental import pallas as pl
from jax.experimental.pallas import tpu as pltpu
from jax.sharding import PartitionSpec as P

HEAD_DIM = 64
STATE = 128
CH = 64
TILE = 2 * CH
GROUP = 4


def swapped(value, axis, apart):
    mask = 2**apart
    pairs = [(source, source ^ mask) for source in range(lax.axis_size(axis))]
    return lax.ppermute(value, axis, pairs)


def dot32(left, right):
    return jnp.dot(left, right, preferred_element_type=jnp.float32)


def spread(cols, quantity, quantities, group, rows=slice(None)):
    parts = []
    count = rows.stop - rows.start if rows.start is not None else cols.shape[1]
    low = lax.broadcasted_iota(jnp.int32, (count, 2 * HEAD_DIM), 1) < HEAD_DIM
    for pair in range(group // 2):
        first, second = (2 * pair) * quantities + quantity, (2 * pair + 1) * quantities + quantity
        parts.append(
            jnp.where(low, cols[0, rows, first : first + 1], cols[0, rows, second : second + 1])
        )
    return jnp.concatenate(parts, axis=1)


def level_grad_kernel(names, group, read_t, grads, cols, out):
    count = len(names)
    for b in range(out.shape[0]):
        scaled = (spread(cols, names.index(("q", b)), count, group) * grads[...]).astype(jnp.bfloat16)
        out[b] = dot32(read_t[...], scaled)


def seg_state_kernel(names, group, write_t, values, cols, out):
    scaled = (spread(cols, names.index("key"), len(names), group) * values[...]).astype(jnp.bfloat16)
    out[...] = dot32(write_t[...], scaled)


def diagonal_terms(names, group, table, cols, rows, operand, rows_of, backward):
    count = len(names)
    position = slice(rows_of, rows_of + TILE)
    own = table[position, position].astype(jnp.float32)
    shape = (TILE, TILE)
    same = (lax.broadcasted_iota(jnp.int32, shape, 0) < CH) == (
        lax.broadcasted_iota(jnp.int32, shape, 1) < CH
    )
    parts = []
    for head in range(group):
        cum_col = cols[0, position, head * count : head * count + 1]
        cum_row = rows[0, 3 * head : 3 * head + 1, position]
        if backward:
            gain = jnp.where(
                same, rows[0, 3 * head + 1 : 3 * head + 2, position], rows[0, 3 * head + 2 : 3 * head + 3, position]
            )
            differ = cum_row - cum_col
        else:
            gain = jnp.where(
                same,
                cols[0, position, head * count + 1 : head * count + 2],
                cols[0, position, head * count + 2 : head * count + 3],
            )
            differ = cum_col - cum_row
        weights = (gain * jnp.exp(jnp.minimum(differ, 0.0)) * own).astype(jnp.bfloat16)
        parts.append(dot32(weights, operand[position, head * HEAD_DIM : (head + 1) * HEAD_DIM]))
    return jnp.concatenate(parts, axis=1)


def local_kernel(names, group, levels, backward, table, proj, operand, states, cols, rows, out):
    count = len(names)
    length = out.shape[0]
    tiles = length // TILE
    sums = []
    for tile in range(tiles):
        position = slice(tile * TILE, (tile + 1) * TILE)
        total = diagonal_terms(names, group, table, cols, rows, operand, tile * TILE, backward)
        if backward:
            total = total + spread(cols, names.index("key"), count, group, position) * dot32(
                proj[position, :], states[...]
            )
        else:
            for b in range(states.shape[0]):
                total = total + spread(cols, names.index(("q", b)), count, group, position) * dot32(
                    proj[position, :], states[b]
                )
        sums.append(total)
    for level in range(2, levels):
        half = CH << (level - 1)
        for start in range(0, length, 2 * half):
            lower, upper = slice(start, start + half), slice(start + half, start + 2 * half)
            source, target = (upper, lower) if backward else (lower, upper)
            inner, outer = ("r", "c") if backward else ("c", "r")
            scaled = (
                spread(cols, names.index((inner, level)), count, group, source) * operand[source, :]
            ).astype(jnp.bfloat16)
            term = spread(cols, names.index((outer, level)), count, group, target) * dot32(
                table[target, source], scaled
            )
            for step in range(half // TILE):
                at = target.start // TILE + step
                sums[at] = sums[at] + term[step * TILE : (step + 1) * TILE]
    for tile in range(tiles):
        out[tile * TILE : (tile + 1) * TILE, :] = sums[tile].astype(out.dtype)


def bit_orders(bits):
    straight = list(range(bits))
    turned = straight[1:2] + straight[:1] + straight[2:]
    return [turned, straight, straight, straight]


def gathered(block, order):
    have = [([0], block)]
    for bit in reversed(order):
        have += [([r ^ 1 << bit for r in marks], swapped(part, "seq", bit)) for marks, part in have]
    return have


def scattered(blocks_t, grads, order):
    half = blocks_t.shape[1] // 2

    def product(part):
        return lax.dot_general(
            part, grads, (((0,), (0,)), ((), ())), preferred_element_type=jnp.float32
        ).astype(jnp.bfloat16)

    send, keep = product(blocks_t[:, half:]), product(blocks_t[:, :half])
    for step, bit in enumerate(order):
        arrived = swapped(send, "seq", bit)
        total = keep.astype(jnp.float32) + arrived.astype(jnp.float32)
        half = total.shape[0] // 2
        if step + 1 == len(order):
            return total.astype(jnp.bfloat16)
        keep, send = total[:half], total[half:].astype(jnp.bfloat16)


def marks_of(order):
    marks = [0]
    for bit in reversed(order):
        marks = marks + [r | 1 << bit for r in marks]
    return marks


def whole_spec(array):
    return pl.BlockSpec(array.shape, lambda i: (0,) * array.ndim)


def column_spec(array, width):
    lead = array.shape[:-1]
    return pl.BlockSpec(lead + (width,), lambda i: (0,) * len(lead) + (i,))


def group_spec(array):
    return pl.BlockSpec((1,) + array.shape[1:], lambda i: (i, 0, 0))


def call(kernel, groups, width, fixed, wide, grouped, out_shape, flops, name):
    out_lead = out_shape.shape[:-1]
    moved = sum(a.size * a.dtype.itemsize for a in (*fixed, *wide, *grouped))
    return pl.pallas_call(
        kernel,
        grid=(groups,),
        in_specs=[whole_spec(a) for a in fixed]
        + [column_spec(a, width) for a in wide]
        + [group_spec(a) for a in grouped],
        out_specs=pl.BlockSpec(out_lead + (width,), lambda i: (0,) * len(out_lead) + (i,)),
        out_shape=out_shape,
        compiler_params=pltpu.CompilerParams(vmem_limit_bytes=40 * 2**20),
        cost_estimate=pl.CostEstimate(flops=flops, bytes_accessed=moved, transcendentals=0),
        name=name,
    )(*fixed, *wide, *grouped)


def per_device(tokens, in_weight, write_proj, read_proj, log_decay, level_gain, out_grad):
    orders = bit_orders(lax.axis_size("seq").bit_length() - 1)
    chunk = in_weight.shape[1] // len(orders)
    pieces = [gathered(in_weight[:, i * chunk : (i + 1) * chunk], order) for i, order in enumerate(orders)]
    both = lax.all_gather(jnp.concatenate([write_proj, read_proj], axis=1), "head", axis=0, tiled=True)
    write_rows, read_rows = both[:, :STATE], both[:, STATE:]
    full_tokens = lax.all_gather(tokens, "head", axis=0, tiled=True)
    tok_len = full_tokens.shape[0]
    head_count = log_decay.shape[0]
    columns = in_weight.shape[1]
    levels = (tok_len // CH).bit_length()
    seq_count = lax.axis_size("seq").bit_length() - 1
    me = lax.axis_index("seq")
    group = GROUP
    groups = head_count // group
    width = group * HEAD_DIM

    upper_ones = (jnp.arange(tok_len)[:, None] <= jnp.arange(tok_len)[None, :]).astype(jnp.float32)
    cumulative = jnp.dot(log_decay, upper_ones, precision=lax.Precision.HIGHEST)
    totals = cumulative[:, -1]
    all_totals = lax.all_gather(totals, "seq", axis=0, tiled=False)

    names = ["cum", "g0", "g1"]
    vectors = [cumulative, level_gain[0], level_gain[1]]
    for level in range(2, levels):
        half = CH << (level - 1)
        blocks = cumulative.reshape(head_count, tok_len // (2 * half), 2 * half)
        middle = blocks[:, :, half - 1 : half]
        after = jnp.exp(jnp.minimum(blocks - middle, 0.0)).reshape(head_count, tok_len)
        before = jnp.exp(jnp.minimum(middle - blocks, 0.0)).reshape(head_count, tok_len)
        names += [("r", level), ("c", level)]
        vectors += [level_gain[level] * after, before]
    names.append("key")
    vectors.append(jnp.exp(totals[:, None] - cumulative))
    grown = jnp.exp(cumulative)
    for b in range(seq_count):
        names.append(("q", b))
        vectors.append(level_gain[levels + b] * grown)
    names = tuple(names)
    count = len(names)
    cols = jnp.stack(vectors, axis=1).reshape(groups, group * count, tok_len).swapaxes(1, 2)
    rows = jnp.stack(vectors[:3], axis=1).reshape(groups, group * 3, tok_len)

    causal = jnp.arange(tok_len)[:, None] >= jnp.arange(tok_len)[None, :]
    scores = jnp.where(causal, dot32(read_rows, write_rows.T), 0.0).astype(jnp.bfloat16)
    scores_t = jnp.where(causal.T, dot32(write_rows, read_rows.T), 0.0).astype(jnp.bfloat16)

    work = 2 * tok_len * STATE * columns
    level_grads = call(
        functools.partial(level_grad_kernel, names, group),
        groups, width, [read_rows.T], [out_grad], [cols],
        jax.ShapeDtypeStruct((seq_count, STATE, columns), jnp.float32), seq_count * work, "level_grads",
    )

    index = jnp.arange(all_totals.shape[0])
    bit_flags = [me >> bit & 1 == 1 for bit in range(seq_count)]

    def per_column(vector):
        return jnp.repeat(vector, HEAD_DIM)[None, :]

    own_decays, partner_decays = [], []
    for bit in range(seq_count):
        for found, block in ((own_decays, me >> bit), (partner_decays, (me >> bit) ^ 1)):
            inside = (index >> bit == block)[:, None]
            found.append(per_column(jnp.exp(jnp.sum(jnp.where(inside, all_totals, 0.0), axis=0))))

    pending = [jnp.where(bit_flags[bit], level_grads[bit], 0.0) for bit in range(seq_count)]
    suffix = jnp.ones((1, columns), jnp.float32)
    state_grad = jnp.zeros((STATE, columns), jnp.float32)
    for bit in range(seq_count):
        partner = swapped(jnp.stack(pending[bit:]).astype(jnp.bfloat16), "seq", bit).astype(jnp.float32)
        is_upper = bit_flags[bit]
        state_grad = state_grad + jnp.where(is_upper, 0.0, suffix * partner[0])
        for later in range(bit + 1, seq_count):
            rest, other = pending[later], partner[later - bit]
            pending[later] = jnp.where(
                is_upper, other + partner_decays[bit] * rest, rest + own_decays[bit] * other
            )
        suffix = jnp.where(is_upper, suffix, suffix * partner_decays[bit])

    local_work = work + 2 * tok_len * tok_len * columns
    values_grad = call(
        functools.partial(local_kernel, names, group, levels, True),
        groups, width, [scores_t, write_rows], [out_grad, state_grad.astype(jnp.bfloat16)], [cols, rows],
        jax.ShapeDtypeStruct((tok_len, columns), jnp.bfloat16), local_work, "backward",
    )
    depth = in_weight.shape[0]
    blocks = [
        lax.dynamic_slice_in_dim(full_tokens, (me ^ r) * depth, depth, axis=1)
        for r in range(lax.axis_size("seq"))
    ]
    parts = []
    for i, order in enumerate(orders):
        marks = marks_of(order)
        ordered = jnp.concatenate([blocks[r] for r in marks], axis=1)
        parts.append(scattered(ordered, values_grad[:, i * chunk : (i + 1) * chunk], order))
    weight_grad = jnp.concatenate(parts, axis=1)

    chunks = []
    for have in pieces:
        total = 0.0
        for marks, part in have:
            for k, r in enumerate(marks):
                total = total + dot32(blocks[r], part[k * depth : (k + 1) * depth])
        chunks.append(total.astype(jnp.bfloat16))
    values = jnp.concatenate(chunks, axis=1)
    block_state = call(
        functools.partial(seg_state_kernel, names, group),
        groups, width, [write_rows.T], [values], [cols],
        jax.ShapeDtypeStruct((STATE, columns), jnp.float32), work, "seg_state",
    )
    prefix = jnp.ones((1, columns), jnp.float32)
    buckets = []
    for bit in range(seq_count):
        partner = swapped(block_state.astype(jnp.bfloat16), "seq", bit).astype(jnp.float32)
        is_upper = bit_flags[bit]
        buckets.append(jnp.where(is_upper, prefix * partner, 0.0).astype(jnp.bfloat16))
        block_state = jnp.where(
            is_upper,
            own_decays[bit] * partner + block_state,
            partner_decays[bit] * block_state + partner,
        )
        prefix = jnp.where(is_upper, partner_decays[bit] * prefix, prefix)
    layer_out = call(
        functools.partial(local_kernel, names, group, levels, False),
        groups, width, [scores, read_rows], [values, jnp.stack(buckets)], [cols, rows],
        jax.ShapeDtypeStruct((tok_len, columns), jnp.bfloat16), local_work, "forward",
    )
    return (layer_out, weight_grad)


def solution(mesh):
    in_specs = (
        P(("seq", "head"), None),
        P("seq", "head"),
        P(("seq", "head"), None),
        P(("seq", "head"), None),
        P("head", "seq"),
        P(None, "head", "seq"),
        P("seq", "head"),
    )
    out_specs = (P("seq", "head"), P("seq", "head"))
    return jax.shard_map(
        per_device, mesh=mesh, in_specs=in_specs, out_specs=out_specs, check_vma=False
    )
```

```python
import functools

import jax
import jax.numpy as jnp
from jax import lax
from jax.experimental import pallas as pl
from jax.experimental.pallas import tpu as pltpu
from jax.sharding import PartitionSpec as P

HEAD_DIM = 64
STATE = 128
CH = 64
TILE = 2 * CH
GROUP = 4


def swapped(value, axis, apart):
    mask = 2**apart
    pairs = [(source, source ^ mask) for source in range(lax.axis_size(axis))]
    return lax.ppermute(value, axis, pairs)


def dot32(left, right):
    return jnp.dot(left, right, preferred_element_type=jnp.float32)


def spread(cols, quantity, quantities, group, rows=slice(None)):
    parts = []
    count = rows.stop - rows.start if rows.start is not None else cols.shape[1]
    low = lax.broadcasted_iota(jnp.int32, (count, 2 * HEAD_DIM), 1) < HEAD_DIM
    for pair in range(group // 2):
        first, second = (2 * pair) * quantities + quantity, (2 * pair + 1) * quantities + quantity
        parts.append(
            jnp.where(low, cols[0, rows, first : first + 1], cols[0, rows, second : second + 1])
        )
    return jnp.concatenate(parts, axis=1)


def level_grad_kernel(names, group, read_t, grads, cols, out):
    count = len(names)
    for b in range(out.shape[0]):
        scaled = (spread(cols, names.index(("q", b)), count, group) * grads[...]).astype(jnp.bfloat16)
        out[b] = dot32(read_t[...], scaled)


def seg_state_kernel(names, group, write_t, values, cols, out):
    scaled = (spread(cols, names.index("key"), len(names), group) * values[...]).astype(jnp.bfloat16)
    out[...] = dot32(write_t[...], scaled)


def diagonal_terms(names, group, table, cols, rows, operand, rows_of, backward):
    count = len(names)
    position = slice(rows_of, rows_of + TILE)
    own = table[position, position].astype(jnp.float32)
    shape = (TILE, TILE)
    same = (lax.broadcasted_iota(jnp.int32, shape, 0) < CH) == (
        lax.broadcasted_iota(jnp.int32, shape, 1) < CH
    )
    parts = []
    for head in range(group):
        cum_col = cols[0, position, head * count : head * count + 1]
        cum_row = rows[0, 3 * head : 3 * head + 1, position]
        if backward:
            gain = jnp.where(
                same, rows[0, 3 * head + 1 : 3 * head + 2, position], rows[0, 3 * head + 2 : 3 * head + 3, position]
            )
            differ = cum_row - cum_col
        else:
            gain = jnp.where(
                same,
                cols[0, position, head * count + 1 : head * count + 2],
                cols[0, position, head * count + 2 : head * count + 3],
            )
            differ = cum_col - cum_row
        weights = (gain * jnp.exp(jnp.minimum(differ, 0.0)) * own).astype(jnp.bfloat16)
        parts.append(dot32(weights, operand[position, head * HEAD_DIM : (head + 1) * HEAD_DIM]))
    return jnp.concatenate(parts, axis=1)


def local_kernel(names, group, levels, backward, table, proj, operand, states, cols, rows, out):
    count = len(names)
    length = out.shape[0]
    tiles = length // TILE
    sums = []
    for tile in range(tiles):
        position = slice(tile * TILE, (tile + 1) * TILE)
        total = diagonal_terms(names, group, table, cols, rows, operand, tile * TILE, backward)
        if backward:
            total = total + spread(cols, names.index("key"), count, group, position) * dot32(
                proj[position, :], states[...]
            )
        else:
            for b in range(states.shape[0]):
                total = total + spread(cols, names.index(("q", b)), count, group, position) * dot32(
                    proj[position, :], states[b]
                )
        sums.append(total)
    for level in range(2, levels):
        half = CH << (level - 1)
        for start in range(0, length, 2 * half):
            lower, upper = slice(start, start + half), slice(start + half, start + 2 * half)
            source, target = (upper, lower) if backward else (lower, upper)
            inner, outer = ("r", "c") if backward else ("c", "r")
            scaled = (
                spread(cols, names.index((inner, level)), count, group, source) * operand[source, :]
            ).astype(jnp.bfloat16)
            term = spread(cols, names.index((outer, level)), count, group, target) * dot32(
                table[target, source], scaled
            )
            for step in range(half // TILE):
                at = target.start // TILE + step
                sums[at] = sums[at] + term[step * TILE : (step + 1) * TILE]
    for tile in range(tiles):
        out[tile * TILE : (tile + 1) * TILE, :] = sums[tile].astype(out.dtype)


def bit_orders(bits):
    straight = list(range(bits))
    turned = straight[1:2] + straight[:1] + straight[2:]
    return [turned, straight, turned, straight]


def gathered(block, order):
    have = [([0], block)]
    for bit in reversed(order):
        have += [([r ^ 1 << bit for r in marks], swapped(part, "seq", bit)) for marks, part in have]
    return have


def scatter_terms(blocks_t, grads):
    half = blocks_t.shape[1] // 2

    def product(part):
        return lax.dot_general(
            part, grads, (((0,), (0,)), ((), ())), preferred_element_type=jnp.float32
        ).astype(jnp.bfloat16)

    return product(blocks_t[:, half:]), product(blocks_t[:, :half])


def scatter_step(send, keep, bit):
    arrived = swapped(send, "seq", bit)
    total = keep.astype(jnp.float32) + arrived.astype(jnp.float32)
    half = total.shape[0] // 2
    return total[half:].astype(jnp.bfloat16), total[:half], total


def marks_of(order):
    marks = [0]
    for bit in reversed(order):
        marks = marks + [r | 1 << bit for r in marks]
    return marks


def whole_spec(array):
    return pl.BlockSpec(array.shape, lambda i: (0,) * array.ndim)


def column_spec(array, width):
    lead = array.shape[:-1]
    return pl.BlockSpec(lead + (width,), lambda i: (0,) * len(lead) + (i,))


def group_spec(array):
    return pl.BlockSpec((1,) + array.shape[1:], lambda i: (i, 0, 0))


def call(kernel, groups, width, fixed, wide, grouped, out_shape, flops, name):
    out_lead = out_shape.shape[:-1]
    moved = sum(a.size * a.dtype.itemsize for a in (*fixed, *wide, *grouped))
    return pl.pallas_call(
        kernel,
        grid=(groups,),
        in_specs=[whole_spec(a) for a in fixed]
        + [column_spec(a, width) for a in wide]
        + [group_spec(a) for a in grouped],
        out_specs=pl.BlockSpec(out_lead + (width,), lambda i: (0,) * len(out_lead) + (i,)),
        out_shape=out_shape,
        compiler_params=pltpu.CompilerParams(vmem_limit_bytes=40 * 2**20),
        cost_estimate=pl.CostEstimate(flops=flops, bytes_accessed=moved, transcendentals=0),
        name=name,
    )(*fixed, *wide, *grouped)


def per_device(tokens, in_weight, write_proj, read_proj, log_decay, level_gain, out_grad):
    both = lax.all_gather(jnp.concatenate([write_proj, read_proj], axis=1), "head", axis=0, tiled=True)
    write_rows, read_rows = both[:, :STATE], both[:, STATE:]
    full_tokens = lax.all_gather(tokens, "head", axis=0, tiled=True)
    tok_len = full_tokens.shape[0]
    head_count = log_decay.shape[0]
    columns = in_weight.shape[1]
    levels = (tok_len // CH).bit_length()
    seq_count = lax.axis_size("seq").bit_length() - 1
    me = lax.axis_index("seq")
    group = GROUP
    groups = head_count // group
    width = group * HEAD_DIM

    upper_ones = (jnp.arange(tok_len)[:, None] <= jnp.arange(tok_len)[None, :]).astype(jnp.float32)
    cumulative = jnp.dot(log_decay, upper_ones, precision=lax.Precision.HIGHEST)
    totals = cumulative[:, -1]
    all_totals = lax.all_gather(totals, "seq", axis=0, tiled=False)
    in_weight, all_totals = lax.optimization_barrier((in_weight, all_totals))
    orders = bit_orders(lax.axis_size("seq").bit_length() - 1)
    chunk = in_weight.shape[1] // len(orders)
    pieces = [gathered(in_weight[:, i * chunk : (i + 1) * chunk], order) for i, order in enumerate(orders)]

    names = ["cum", "g0", "g1"]
    vectors = [cumulative, level_gain[0], level_gain[1]]
    for level in range(2, levels):
        half = CH << (level - 1)
        blocks = cumulative.reshape(head_count, tok_len // (2 * half), 2 * half)
        middle = blocks[:, :, half - 1 : half]
        after = jnp.exp(jnp.minimum(blocks - middle, 0.0)).reshape(head_count, tok_len)
        before = jnp.exp(jnp.minimum(middle - blocks, 0.0)).reshape(head_count, tok_len)
        names += [("r", level), ("c", level)]
        vectors += [level_gain[level] * after, before]
    names.append("key")
    vectors.append(jnp.exp(totals[:, None] - cumulative))
    grown = jnp.exp(cumulative)
    for b in range(seq_count):
        names.append(("q", b))
        vectors.append(level_gain[levels + b] * grown)
    names = tuple(names)
    count = len(names)
    cols = jnp.stack(vectors, axis=1).reshape(groups, group * count, tok_len).swapaxes(1, 2)
    rows = jnp.stack(vectors[:3], axis=1).reshape(groups, group * 3, tok_len)

    causal = jnp.arange(tok_len)[:, None] >= jnp.arange(tok_len)[None, :]
    scores = jnp.where(causal, dot32(read_rows, write_rows.T), 0.0).astype(jnp.bfloat16)
    scores_t = jnp.where(causal.T, dot32(write_rows, read_rows.T), 0.0).astype(jnp.bfloat16)

    work = 2 * tok_len * STATE * columns
    level_grads = call(
        functools.partial(level_grad_kernel, names, group),
        groups, width, [read_rows.T], [out_grad], [cols],
        jax.ShapeDtypeStruct((seq_count, STATE, columns), jnp.float32), seq_count * work, "level_grads",
    )

    index = jnp.arange(all_totals.shape[0])
    bit_flags = [me >> bit & 1 == 1 for bit in range(seq_count)]

    def per_column(vector):
        return jnp.repeat(vector, HEAD_DIM)[None, :]

    own_decays, partner_decays = [], []
    for bit in range(seq_count):
        for found, block in ((own_decays, me >> bit), (partner_decays, (me >> bit) ^ 1)):
            inside = (index >> bit == block)[:, None]
            found.append(per_column(jnp.exp(jnp.sum(jnp.where(inside, all_totals, 0.0), axis=0))))

    pending = [jnp.where(bit_flags[bit], level_grads[bit], 0.0) for bit in range(seq_count)]
    suffix = jnp.ones((1, columns), jnp.float32)
    state_grad = jnp.zeros((STATE, columns), jnp.float32)
    for bit in range(seq_count):
        partner = swapped(jnp.stack(pending[bit:]).astype(jnp.bfloat16), "seq", bit).astype(jnp.float32)
        is_upper = bit_flags[bit]
        state_grad = state_grad + jnp.where(is_upper, 0.0, suffix * partner[0])
        for later in range(bit + 1, seq_count):
            rest, other = pending[later], partner[later - bit]
            pending[later] = jnp.where(
                is_upper, other + partner_decays[bit] * rest, rest + own_decays[bit] * other
            )
        suffix = jnp.where(is_upper, suffix, suffix * partner_decays[bit])

    local_work = work + 2 * tok_len * tok_len * columns
    values_grad = call(
        functools.partial(local_kernel, names, group, levels, True),
        groups, width, [scores_t, write_rows], [out_grad, state_grad.astype(jnp.bfloat16)], [cols, rows],
        jax.ShapeDtypeStruct((tok_len, columns), jnp.bfloat16), local_work, "backward",
    )
    depth = in_weight.shape[0]
    blocks = [
        lax.dynamic_slice_in_dim(full_tokens, (me ^ r) * depth, depth, axis=1)
        for r in range(lax.axis_size("seq"))
    ]
    parts = []
    for i, order in enumerate(orders):
        marks = marks_of(order)
        ordered = jnp.concatenate([blocks[r] for r in marks], axis=1)
        send, keep = scatter_terms(ordered, values_grad[:, i * chunk : (i + 1) * chunk])
        parts.append(scatter_step(send, keep, order[0]))
    second_sends = [part[0] for part in parts]
    for step in range(1, seq_count):
        parts = [
            scatter_step(part[0], part[1], order[step]) for part, order in zip(parts, orders)
        ]
    weight_grad = jnp.concatenate([part[2].astype(jnp.bfloat16) for part in parts], axis=1)

    chunks = []
    for have in pieces:
        total = 0.0
        for marks, part in have:
            for k, r in enumerate(marks):
                total = total + dot32(blocks[r], part[k * depth : (k + 1) * depth])
        chunks.append(total.astype(jnp.bfloat16))
    values = jnp.concatenate(chunks, axis=1)
    block_state = call(
        functools.partial(seg_state_kernel, names, group),
        groups, width, [write_rows.T], [values], [cols],
        jax.ShapeDtypeStruct((STATE, columns), jnp.float32), work, "seg_state",
    )
    prefix = jnp.ones((1, columns), jnp.float32)
    buckets = []
    for bit in range(seq_count):
        partner = swapped(block_state.astype(jnp.bfloat16), "seq", bit).astype(jnp.float32)
        is_upper = bit_flags[bit]
        buckets.append(jnp.where(is_upper, prefix * partner, 0.0).astype(jnp.bfloat16))
        block_state = jnp.where(
            is_upper,
            own_decays[bit] * partner + block_state,
            partner_decays[bit] * block_state + partner,
        )
        prefix = jnp.where(is_upper, partner_decays[bit] * prefix, prefix)
    values_late = lax.optimization_barrier((values, *second_sends))[0]
    layer_out = call(
        functools.partial(local_kernel, names, group, levels, False),
        groups, width, [scores, read_rows], [values_late, jnp.stack(buckets)], [cols, rows],
        jax.ShapeDtypeStruct((tok_len, columns), jnp.bfloat16), local_work, "forward",
    )
    return (layer_out, weight_grad)


def solution(mesh):
    in_specs = (
        P(("seq", "head"), None),
        P("seq", "head"),
        P(("seq", "head"), None),
        P(("seq", "head"), None),
        P("head", "seq"),
        P(None, "head", "seq"),
        P("seq", "head"),
    )
    out_specs = (P("seq", "head"), P("seq", "head"))
    return jax.shard_map(
        per_device, mesh=mesh, in_specs=in_specs, out_specs=out_specs, check_vma=False
    )
```
